128 devices in a mesh: col: 16 (over y_hi, x, core), row: 8 (over z, y_lo).
Axes of the slice: x: 4, y: 4 (y_hi: 2, y_lo: 2; y = y_hi * 2 + y_lo), z: 4, core: 2. Of those that a mesh axis runs over, the one named last changes fastest.
Arguments:
- weight: bfloat16 [4096, 16384], P('row', 'col'), may hold values from -10 to 10
Outputs:
- codes: bfloat16 [4096, 16384], P('row')
- scales: float32 [4096], P('row')
The draws below stay inside these ranges and needn't reach their ends.
All inputs are finite; a program needn't handle non-finite values. Where the reference program divides by a largest or mean magnitude, that divisor is 1e-20 or more.
Results may differ from the reference program's by a relative error of at most 0.015.
Values may be sent and summed in bfloat16 or wider, within the bound.
No kernel may reach another device: no remote copies, remote signals or barrier semaphores. Data moves between devices by JAX's collectives and lax.ppermute only.
A program may use at most 128 MiB of HBM per device.

```python
import jax
import jax.numpy as jnp
from jax import lax

D = 16384
ROWS = 4096
BLK = 64
N_ROW = 8


def draw_weight(key, part):
    key = jax.random.fold_in(key, 7)
    noise_key, row_key, col_key = jax.random.split(key, 3)
    noise = jax.random.normal(noise_key, (ROWS, D), jnp.float32)
    row_scale = jnp.exp(jax.random.uniform(row_key, (ROWS, 1), jnp.float32, 0.0, 2.3))
    noise = jnp.clip(noise, -3.0, 3.0)
    col_scale = jnp.exp(jax.random.uniform(col_key, (1, D), jnp.float32, 0.0, 2.3))
    values = jnp.clip(noise * row_scale * col_scale * 0.02, -10.0, 10.0)
    return values.astype(jnp.bfloat16)


def setup_inputs(seed: int = 0) -> dict:
    streams_of = jax.random.split(jax.random.key(seed), 2)
    return {
        "weight": draw_weight(jax.random.fold_in(streams_of[1], 71), 0),
    }


def hadamard(order):
    table = jnp.ones((1, 1), jnp.float32)
    while table.shape[0] < order:
        table = jnp.concatenate([jnp.concatenate([table, table], 1), jnp.concatenate([table, -table], 1)], 0)
    return table

def reference(weight):
    ordered = weight.reshape(N_ROW, N_ROW, BLK, D).transpose(1, 0, 2, 3).reshape(ROWS, D)
    outer = D // 128
    inner_table = hadamard(128).astype(jnp.bfloat16)
    outer_table = hadamard(outer)
    partial_rot = jnp.dot(ordered.reshape(ROWS * outer, 128), inner_table, preferred_element_type=jnp.float32)
    partial_rot = partial_rot.reshape(ROWS, outer, 128)
    rotated = jnp.einsum('rab,ac->rcb', partial_rot, outer_table, precision=lax.Precision.HIGHEST)
    rotated = rotated.reshape(ROWS, D) / jnp.sqrt(jnp.float32(D))
    scales = lax.optimization_barrier(jnp.max(jnp.abs(rotated), axis=1)) + 1e-06
    codes = (rotated / scales[:, None]).astype(jnp.bfloat16)
    return (codes, scales)
```

```python
import functools

import jax
import jax.numpy as jnp
import numpy as np
from jax import lax
from jax.experimental import pallas as pl
from jax.experimental.pallas import tpu as pltpu
from jax.sharding import PartitionSpec as P

UNIT = 16
BASE = 256
LANES = 256

XA, XB, YH = 1, 3, 4

CHUNKS = (
    (3, (YH, XA, XB)),
    (3, (XA, XB, YH)),
    (3, (XB, YH, XA)),
    (2, (YH, XA, XB)),
    (2, (XA, XB, YH)),
    (3, (XB, YH, XA)),
)


def hadamard(order):
    table = np.ones((1, 1), np.float32)
    while table.shape[0] < order:
        table = np.block([[table, table], [table, -table]])
    return table


def swapped(value, axis, mask):
    pairs = [(source, source ^ mask) for source in range(lax.axis_size(axis))]
    return lax.ppermute(value, axis, pairs)


def butterfly(parts):
    parts = list(parts)
    span = 1
    while span < len(parts):
        for i in range(len(parts)):
            if not i & span:
                a, b = parts[i], parts[i | span]
                parts[i], parts[i | span] = a + b, a - b
        span *= 2
    return parts


def first_kernel(core_ref, own_ref, got_ref, table_ref, out_ref):
    sign = jnp.where(core_ref[0] == 0, 1.0, -1.0).astype(jnp.float32)
    cols = own_ref.shape[-1]
    rows = own_ref.shape[0] * own_ref.shape[1]
    table = table_ref[...]

    def rotated(ref):
        value = ref[...].reshape(rows, cols)
        return butterfly(
            jnp.dot(value[:, c : c + BASE], table, preferred_element_type=jnp.float32)
            for c in range(0, cols, BASE)
        )

    shape = own_ref.shape[:2] + (BASE,)
    for i, (a, b) in enumerate(zip(rotated(own_ref), rotated(got_ref))):
        out_ref[:, :, i * BASE : (i + 1) * BASE] = (a + b).astype(out_ref.dtype).reshape(shape)
        out_ref[:, :, cols + i * BASE : cols + (i + 1) * BASE] = (
            ((a - b) * sign).astype(out_ref.dtype).reshape(shape)
        )


def first_rotation(weight, got, core):
    blocks, half, cols = got.shape
    per = blocks // 4
    grid = pltpu.PrefetchScalarGridSpec(
        num_scalar_prefetch=1,
        grid=(4,),
        in_specs=[
            pl.BlockSpec((per, half, cols), lambda g, core: (g, core[0], 0)),
            pl.BlockSpec((per, half, cols), lambda g, core: (g, 0, 0)),
            pl.BlockSpec((BASE, BASE), lambda g, core: (0, 0)),
        ],
        out_specs=pl.BlockSpec((per, half, 2 * cols), lambda g, core: (g, 0, 0)),
    )
    return pl.pallas_call(
        first_kernel,
        grid_spec=grid,
        out_shape=jax.ShapeDtypeStruct((blocks, half, 2 * cols), weight.dtype),
        compiler_params=pltpu.CompilerParams(vmem_limit_bytes=16 * 2**20),
        cost_estimate=pl.CostEstimate(
            flops=4 * blocks * half * cols * BASE,
            bytes_accessed=8 * blocks * half * cols,
            transcendentals=0,
        ),
        name="first_rotation",
    )(core, weight, got, jnp.asarray(hadamard(BASE), weight.dtype))


def last_kernel(order, norm, where_ref, c2, r2, r3a, r3b, *rest):
    out_ref, send_ref, scale_ref, work = rest[-4:]
    d1, d2, d3 = order
    place = {}
    for ref, base in ((c2, 0), (r2, d2), (r3a, d3), (r3b, d3 ^ d2)):
        place[base] = (ref, 0)
        place[base ^ d1] = (ref, 1)
    groups = len(place)
    cols = c2.shape[-1]
    peak = None
    for c in range(0, cols, LANES):
        parts = butterfly(
            place[i][0][place[i][1], :, c : c + LANES].astype(jnp.float32) for i in range(groups)
        )
        for k, part in enumerate(parts):
            work[k, :, c : c + LANES] = part
            part = jnp.abs(part)
            peak = part if peak is None else jnp.maximum(peak, part)
    scale = jnp.max(peak, axis=1, keepdims=True) * norm + 1e-06
    scale_ref[...] = jnp.broadcast_to(scale, scale_ref.shape)
    factor = norm / scale
    me = where_ref[1]
    for k in range(groups):
        both = me & k
        odd = (both ^ (both >> 1) ^ (both >> 2)) & 1
        signed = factor * jnp.where(odd == 0, 1.0, -1.0).astype(jnp.float32)
        for c in range(0, cols, LANES):
            value = (work[k, :, c : c + LANES] * signed).astype(out_ref.dtype)
            out_ref[:, k * cols + c : k * cols + c + LANES] = value
            send_ref[:, k * cols + c : k * cols + c + LANES] = value


def place_of(unit, core, units_half):
    return (unit // units_half) * (2 * units_half) + core * units_half + unit % units_half


def last_rotation(start, units, units_half, order, norm, where, shards, out, full):
    _, rows, cols = shards[0].shape
    groups = 8
    wide = groups * cols
    in_specs = [pl.BlockSpec((2, UNIT, cols), lambda g, where: (0, g, 0))] * 4
    operands = [where, *shards]
    aliases = {}
    if out is not None:
        in_specs.append(pl.BlockSpec(memory_space=pl.ANY))
        operands.append(out)
        aliases = {5: 0}
    grid = pltpu.PrefetchScalarGridSpec(
        num_scalar_prefetch=1,
        grid=(units,),
        in_specs=in_specs,
        out_specs=[
            pl.BlockSpec(
                (UNIT, wide), lambda g, where: (place_of(start + g, where[0], units_half), 0)
            ),
            pl.BlockSpec((UNIT, wide), lambda g, where: (g, 0)),
            pl.BlockSpec((UNIT, 128), lambda g, where: (g, 0)),
        ],
        scratch_shapes=[pltpu.VMEM((groups, UNIT, cols), jnp.float32)],
    )
    return pl.pallas_call(
        functools.partial(last_kernel, order, norm),
        grid_spec=grid,
        out_shape=[
            jax.ShapeDtypeStruct((full, wide), shards[0].dtype),
            jax.ShapeDtypeStruct((rows, wide), shards[0].dtype),
            jax.ShapeDtypeStruct((rows, 128), jnp.float32),
        ],
        input_output_aliases=aliases,
        compiler_params=pltpu.CompilerParams(vmem_limit_bytes=16 * 2**20),
        cost_estimate=pl.CostEstimate(
            flops=8 * rows * wide, bytes_accessed=6 * rows * wide, transcendentals=0
        ),
        name="last_rotation",
    )(*operands)


def store_kernel(where_ref, got_ref, out_in, out_ref):
    out_ref[...] = got_ref[...]


def store(start, units, units_half, where, got, out):
    rows, wide = got.shape
    grid = pltpu.PrefetchScalarGridSpec(
        num_scalar_prefetch=1,
        grid=(units,),
        in_specs=[
            pl.BlockSpec((UNIT, wide), lambda g, where: (g, 0)),
            pl.BlockSpec(memory_space=pl.ANY),
        ],
        out_specs=pl.BlockSpec(
            (UNIT, wide), lambda g, where: (place_of(start + g, 1 - where[0], units_half), 0)
        ),
    )
    return pl.pallas_call(
        store_kernel,
        grid_spec=grid,
        out_shape=jax.ShapeDtypeStruct(out.shape, out.dtype),
        input_output_aliases={2: 0},
        compiler_params=pltpu.CompilerParams(vmem_limit_bytes=16 * 2**20),
        cost_estimate=pl.CostEstimate(flops=0, bytes_accessed=4 * rows * wide, transcendentals=0),
        name="store_codes",
    )(where, got, out)


def local(weight):
    position = lax.axis_index("col")
    core = position % 2
    rows, cols = weight.shape
    blocks = lax.axis_size("row")
    block = rows // blocks
    half = block // 2
    norm = 1.0 / float(np.sqrt(cols * lax.axis_size("col")))

    weight = weight.reshape(blocks, block, cols)
    send = lax.dynamic_slice_in_dim(weight, (1 - core) * half, half, axis=1)
    got = swapped(send, "col", 1)
    part = first_rotation(weight, got, core.reshape(1))
    part = lax.all_to_all(part, "row", split_axis=0, concat_axis=0, tiled=True)
    part = part.reshape(blocks * half, 2 * cols)

    def moved(value, step):
        return swapped(value, "col", 2 * step)

    state = []
    start = 0
    for units, order in CHUNKS:
        state.append((start, units, order, part[start * UNIT : (start + units) * UNIT]))
        start += units
    firsts = [moved(own, order[0]) for _, _, order, own in state]
    pairs = [jnp.stack([own, got]) for (_, _, _, own), got in zip(state, firsts)]
    seconds = [moved(pair, order[1]) for (_, _, order, _), pair in zip(state, pairs)]
    thirds = [
        (moved(pair, order[2]), moved(second, order[2]))
        for (_, _, order, _), pair, second in zip(state, pairs, seconds)
    ]

    where = jnp.stack([core, position // 2])
    units_half = half // UNIT
    codes = None
    sent, scales = [], []
    for (start, units, order, _), pair, second, third in zip(state, pairs, seconds, thirds):
        codes, send, scale = last_rotation(
            start, units, units_half, order, norm, where, (pair, second, *third), codes, rows
        )
        sent.append(swapped(send, "col", 1))
        scales.append(scale[:, 0])
    for (start, units, _, _), got in zip(state, sent):
        codes = store(start, units, units_half, where, got, codes)
    mine = jnp.concatenate(scales)
    other = swapped(mine, "col", 1)
    low = jnp.where(core == 0, mine, other).reshape(blocks, half)
    high = jnp.where(core == 0, other, mine).reshape(blocks, half)
    return codes, jnp.concatenate([low, high], axis=1).reshape(rows)


def solution(mesh):
    return jax.shard_map(
        local,
        mesh=mesh,
        in_specs=(P("row", "col"),),
        out_specs=(P("row", None), P("row")),
        check_vma=False,
    )
```

```python
import functools

import jax
import jax.numpy as jnp
import numpy as np
from jax import lax
from jax.experimental import pallas as pl
from jax.experimental.pallas import tpu as pltpu
from jax.sharding import PartitionSpec as P

UNIT = 16
LANES = 256
BASE = 256
EXTRA = 128
GROUPS = 8
VMEM_LIMIT = 12 * 2**20
WORTH = pl.CostEstimate(flops=2*10**10, bytes_accessed=1, transcendentals=0)

STEPS = {"a": 1, "b": 3, "y": 4}


CHUNKS = (
    ((0,), "bay"),
    ((2, 6), "bay"),
    ((1,), "yba"),
    ((4,), "ayb"),
    ((3, 7), "yba"),
    ((5,), "yab"),
)

PLAN = (
    "z2", "m2", "z6", "g0", "g0", "z4", "g1", "m4", "g3", "g2", "g1", "m5", "g4", "g3", "g5",
    "g0", "g2", "g1", "g3", "g4", "g5", "k0", "k2", "k3", "k5r0", "k1", "k4r35", "r142",
)


def swapped(value, axis, mask):
    pairs = [(source, source ^ mask) for source in range(lax.axis_size(axis))]
    return lax.ppermute(value, axis, pairs)


def from_neighbours(value):
    height = lax.axis_size("row")
    far = 2 * STEPS["y"] * height + 1
    pairs = [(source, source ^ far) for source in range(lax.axis_size("col") * height)]
    return swapped(value, "row", 1), lax.ppermute(value, ("col", "row"), pairs)


def butterfly(parts):
    parts = list(parts)
    span = 1
    while span < len(parts):
        for i in range(len(parts)):
            if not i & span:
                a, b = parts[i], parts[i | span]
                parts[i], parts[i | span] = a + b, a - b
        span *= 2
    return parts


def whole(space=pltpu.VMEM):
    return pl.BlockSpec(memory_space=space)


def odd_bits(value, bits):
    total = value
    for bit in range(1, bits):
        total = total ^ (value >> bit)
    return total & 1


def first_kernel(where_ref, own_ref, got_ref, out_ref):
    sign = jnp.where(where_ref[0] == 0, 1.0, -1.0).astype(jnp.float32)
    me = where_ref[2]
    blocks, half, cols = got_ref.shape
    shape = (BASE, BASE)
    both = lax.broadcasted_iota(jnp.int32, shape, 0) & lax.broadcasted_iota(jnp.int32, shape, 1)
    both = both ^ (both >> 4)
    both = both ^ (both >> 2)
    both = both ^ (both >> 1)
    table = (1 - 2 * (both & 1)).astype(jnp.float32).astype(jnp.bfloat16)

    def rotated(value):
        value = value.reshape(blocks * half, cols)
        return butterfly(
            jnp.dot(value[:, c : c + BASE], table, preferred_element_type=jnp.float32)
            for c in range(0, cols, BASE)
        )

    for i, (a, b) in enumerate(zip(rotated(own_ref[...]), rotated(got_ref[...]))):
        low = (a + b).astype(out_ref.dtype)
        high = ((a - b) * sign).astype(out_ref.dtype)
        for block in range(blocks):
            rows = slice(block * half, (block + 1) * half)
            out_ref[block ^ me, :, i * BASE : (i + 1) * BASE] = low[rows]
            out_ref[block ^ me, :, cols + i * BASE : cols + (i + 1) * BASE] = high[rows]


def first_rotation(where, own, got):
    blocks, half, cols = got.shape
    return pl.pallas_call(
        first_kernel,
        in_specs=[whole(pltpu.SMEM), whole(), whole()],
        out_specs=whole(),
        out_shape=jax.ShapeDtypeStruct((blocks, half, 2 * cols), got.dtype),
        compiler_params=pltpu.CompilerParams(vmem_limit_bytes=VMEM_LIMIT),
        cost_estimate=WORTH,
        name="first_rotation",
    )(where, own, got)


def rotate(order, norm, where_ref, held_ref, got_ref, send_ref, scale_ref, work):
    d1, d2, d3 = order
    place = {}
    for ref, base in ((held_ref, 0), (got_ref, d3)):
        for j, other in enumerate((0, d1, d2, d2 ^ d1)):
            place[base ^ other] = (ref, j)
    cols = held_ref.shape[-1]
    me = where_ref[1]

    def step(unit, carry):
        rows = pl.ds(pl.multiple_of(unit * UNIT, UNIT), UNIT)
        peak = None
        for c in range(0, cols, LANES):
            parts = butterfly(
                place[i][0][place[i][1], rows, c : c + LANES].astype(jnp.float32)
                for i in range(GROUPS)
            )
            for k, part in enumerate(parts):
                work[k, :, c : c + LANES] = part
                part = jnp.abs(part)
                peak = part if peak is None else jnp.maximum(peak, part)
        scale = jnp.max(peak, axis=1, keepdims=True) * norm + 1e-06
        scale_ref[rows, :] = jnp.broadcast_to(scale, (UNIT, EXTRA))
        factor = norm / scale
        for k in range(GROUPS):
            signed = factor * jnp.where(odd_bits(me & k, 3) == 0, 1.0, -1.0).astype(jnp.float32)
            for c in range(0, cols, LANES):
                value = (work[k, :, c : c + LANES] * signed).astype(send_ref.dtype)
                send_ref[rows, k * cols + c : k * cols + c + LANES] = value
        high = scale.astype(jnp.bfloat16).astype(jnp.float32)
        mid = (scale - high).astype(jnp.bfloat16).astype(jnp.float32)
        low = scale - high - mid
        lane = lax.broadcasted_iota(jnp.int32, (UNIT, EXTRA), 1)
        terms = jnp.where(lane == 0, high, jnp.where(lane == 1, mid, low))
        send_ref[rows, GROUPS * cols :] = terms.astype(send_ref.dtype)
        return carry

    lax.fori_loop(0, held_ref.shape[1] // UNIT, step, 0)


def places(where_ref, pieces, half, side):
    core = where_ref[0] if side == 0 else 1 - where_ref[0]
    for j, piece in enumerate(pieces):
        start = (where_ref[2] ^ piece) * (2 * half) + core * half
        yield slice(j * half, (j + 1) * half), pl.ds(pl.multiple_of(start, half), half)


def codes_kernel(order, norm, stored, half, earlier, chained, where_ref, *refs):
    refs = list(refs)

    def take(count):
        taken, refs[:] = refs[:count], refs[count:]
        return taken

    inputs = take(2 if order else 0)
    pairs = [take(2) for _ in stored]
    scales = take(len(earlier))
    take(1 if chained else 0)
    outputs = take(2 if order else 0)
    copies = []
    if stored:
        (out_ref,) = take(1)
        wide = out_ref.shape[1]
        got_scale_refs = take(1 if earlier else len(stored))
        sems = refs[-1]
        for pieces, pair in zip(stored, pairs):
            for side, ref in enumerate(pair):
                for rows, place in places(where_ref, pieces, half, side):
                    copies.append(
                        pltpu.make_async_copy(
                            ref.at[rows, pl.ds(0, wide)], out_ref.at[place], sems.at[len(copies)]
                        )
                    )
    for copy in copies:
        copy.start()
    got_scales = []
    for _, got_ref in pairs:
        terms = got_ref[:, wide:].astype(jnp.float32)
        scale = (terms[:, :1] + terms[:, 1:2]) + terms[:, 2:3]
        got_scales.append(jnp.broadcast_to(scale, (scale.shape[0], EXTRA)))
    if order:
        rotate(order, norm, where_ref, *inputs, *outputs, refs[0])
    if earlier:
        table = refs[0]
        for (pieces, side), ref in zip(earlier, scales):
            for rows, place in places(where_ref, pieces, half, side):
                table[place, :] = ref[rows, :]
        for pieces, scale in zip(stored, got_scales):
            for rows, place in places(where_ref, pieces, half, 1):
                table[place, :] = scale[rows]
        shape = (EXTRA, EXTRA)
        row, lane = (lax.broadcasted_iota(jnp.int32, shape, axis) for axis in range(2))
        (scale_ref,) = got_scale_refs
        for q in range(scale_ref.shape[0]):
            block = table[q * EXTRA : (q + 1) * EXTRA, :]
            line = jnp.sum(jnp.where(row == lane, block, 0.0), axis=0, keepdims=True)
            scale_ref[q : q + 1, :] = line
    elif stored:
        for ref, scale in zip(got_scale_refs, got_scales):
            ref[...] = scale
    for copy in copies:
        copy.wait()


def codes_call(order, norm, inputs, stored, pairs, earlier, scales, out, where, half, full):
    dtype = jnp.bfloat16
    operands = [where, *inputs]
    for pair in pairs:
        operands.extend(pair)
    operands.extend(scales)
    in_specs = [whole(pltpu.SMEM)] + [whole()] * (len(operands) - 1)
    out_specs, out_shape, scratch, aliases = [], [], [], {}
    moved = 0
    if order:
        _, rows, cols = inputs[0].shape
        moved = rows // half
        out_specs += [whole(), whole()]
        out_shape += [
            jax.ShapeDtypeStruct((rows, GROUPS * cols + EXTRA), dtype),
            jax.ShapeDtypeStruct((rows, EXTRA), jnp.float32),
        ]
        scratch.append(pltpu.VMEM((GROUPS, UNIT, cols), jnp.float32))
    if earlier:
        scratch.append(pltpu.VMEM((full, EXTRA), jnp.float32))
    if stored:
        if out is not None:
            aliases = {len(operands): len(out_shape)}
            in_specs.append(whole(pl.ANY))
            operands.append(out)
        out_specs.append(whole(pl.ANY))
        out_shape.append(jax.ShapeDtypeStruct((full, pairs[0][0].shape[1] - EXTRA), dtype))
        heights = [full // EXTRA] if earlier else [own.shape[0] for own, _ in pairs]
        out_specs += [whole()] * len(heights)
        out_shape += [jax.ShapeDtypeStruct((rows, EXTRA), jnp.float32) for rows in heights]
        scratch.append(pltpu.SemaphoreType.DMA((2 * sum(len(pieces) for pieces in stored),)))
    return pl.pallas_call(
        functools.partial(codes_kernel, order, norm, stored, half, earlier, bool(aliases)),
        in_specs=in_specs,
        out_specs=out_specs,
        out_shape=out_shape,
        scratch_shapes=scratch,
        input_output_aliases=aliases,
        compiler_params=pltpu.CompilerParams(vmem_limit_bytes=VMEM_LIMIT),
        cost_estimate=WORTH,
        name=f"rotate{moved}_store{sum(len(pieces) for pieces in stored)}",
    )(*operands)


def local(weight):
    position = lax.axis_index("col")
    core = position % 2
    row = lax.axis_index("row")
    where = jnp.stack([core, position // 2, row])
    rows, cols = weight.shape
    blocks = lax.axis_size("row")
    block = rows // blocks
    half = block // 2
    norm = 1.0 / float(np.sqrt(cols * lax.axis_size("col")))

    weight = weight.reshape(blocks, block, cols)
    send = lax.dynamic_slice_in_dim(weight, (1 - core) * half, half, axis=1)
    own = lax.dynamic_slice_in_dim(weight, core * half, half, axis=1)
    part = first_rotation(where, own, swapped(send, "col", 1))

    token = part

    def after(value):
        return lax.optimization_barrier((value, token))[0]

    pieces = {0: part[0], 1: part[1]}
    held, got, taken = {}, {}, {}
    scales = {}
    codes = None
    for step in PLAN:
        kind, i = step[0], int(step[1])
        if kind == "z":
            token = after(part[i : i + 2])
            pair = swapped(token, "row", i)
            pieces[i], pieces[i + 1] = pair[0], pair[1]
            continue
        names, order = CHUNKS[i] if kind != "r" else ((), ())
        order = [STEPS[name] for name in order]
        if kind == "m":
            token = after(jnp.concatenate([pieces[name] for name in names])[None])
            held[i], got[i] = from_neighbours(token)
            taken[i] = 1
        elif kind == "g":
            turn = taken.get(i, 0)
            taken[i] = turn + 1
            if turn == 0:
                held[i] = jnp.concatenate([pieces[name] for name in names])[None]
            else:
                held[i] = jnp.concatenate([held[i], got[i]])
            token = held[i] = after(held[i])
            got[i] = swapped(token, "col", 2 * order[turn])
        else:
            ready = [int(name) for name in step.partition("r")[2]]
            stored = [CHUNKS[c][0] for c in ready]
            pairs = [(held[c], got[c]) for c in ready]
            earlier = dict(scales) if step == PLAN[-1] else {}
            inputs = ()
            if kind == "k":
                inputs = (held[i], after(got[i]))
            else:
                pairs[-1] = (pairs[-1][0], after(pairs[-1][1]))
            made = codes_call(
                order,
                norm,
                inputs,
                stored,
                pairs,
                list(earlier),
                list(earlier.values()),
                codes,
                where,
                half,
                rows,
            )
            if kind == "k":
                held[i], scales[names, 0], *made = made
                got[i] = swapped(held[i], "col", 1)
                token = held[i]
            if ready:
                codes, *made = made
                for pieces_of, scale in zip(stored, made):
                    scales[pieces_of, 1] = scale

    return codes, made[0].reshape(rows)


def solution(mesh):
    return jax.shard_map(
        local,
        mesh=mesh,
        in_specs=(P("row", "col"),),
        out_specs=(P("row", None), P("row")),
        check_vma=False,
    )
```

```python
import functools

import jax
import jax.numpy as jnp
import numpy as np
from jax import lax
from jax.experimental import pallas as pl
from jax.experimental.pallas import tpu as pltpu
from jax.sharding import PartitionSpec as P

UNIT = 16
LANES = 256
BASE = 256
EXTRA = 128
GROUPS = 8
VMEM_LIMIT = 12 * 2**20
WORTH = pl.CostEstimate(flops=2*10**10, bytes_accessed=1, transcendentals=0)

STEPS = {"a": 1, "b": 3, "y": 4}


CHUNKS = (
    ((0,), "aby"),
    ((2, 6), "bay"),
    ((1,), "yba"),
    ((4,), "ayb"),
    ((3, 7), "yba"),
    ((5,), "yab"),
)

PLAN = (
    "z2", "m2", "z6", "z4", "g1", "g0", "g1", "g0", "m4", "g3", "m5", "g2", "g3", "g5", "g4",
    "g0", "g2", "g3", "g4", "g1", "g5", "k0", "k2o0", "k5o2", "k3o5", "k4o3r20", "k1o4r35",
    "o1r4", "r1",
)


def swapped(value, axis, mask):
    pairs = [(source, source ^ mask) for source in range(lax.axis_size(axis))]
    return lax.ppermute(value, axis, pairs)


def from_neighbours(value):
    height = lax.axis_size("row")
    far = 2 * STEPS["y"] * height + 1
    pairs = [(source, source ^ far) for source in range(lax.axis_size("col") * height)]
    return swapped(value, "row", 1), lax.ppermute(value, ("col", "row"), pairs)


def butterfly(parts):
    parts = list(parts)
    span = 1
    while span < len(parts):
        for i in range(len(parts)):
            if not i & span:
                a, b = parts[i], parts[i | span]
                parts[i], parts[i | span] = a + b, a - b
        span *= 2
    return parts


def whole(space=pltpu.VMEM):
    return pl.BlockSpec(memory_space=space)


def odd_bits(value, bits):
    total = value
    for bit in range(1, bits):
        total = total ^ (value >> bit)
    return total & 1


def first_kernel(where_ref, own_ref, got_ref, out_ref):
    sign = jnp.where(where_ref[0] == 0, 1.0, -1.0).astype(jnp.float32)
    me = where_ref[2]
    blocks, half, cols = got_ref.shape
    shape = (BASE, BASE)
    both = lax.broadcasted_iota(jnp.int32, shape, 0) & lax.broadcasted_iota(jnp.int32, shape, 1)
    both = both ^ (both >> 4)
    both = both ^ (both >> 2)
    both = both ^ (both >> 1)
    table = (1 - 2 * (both & 1)).astype(jnp.float32).astype(jnp.bfloat16)

    def rotated(value):
        value = value.reshape(blocks * half, cols)
        return butterfly(
            jnp.dot(value[:, c : c + BASE], table, preferred_element_type=jnp.float32)
            for c in range(0, cols, BASE)
        )

    for i, (a, b) in enumerate(zip(rotated(own_ref[...]), rotated(got_ref[...]))):
        low = (a + b).astype(out_ref.dtype)
        high = ((a - b) * sign).astype(out_ref.dtype)
        for block in range(blocks):
            rows = slice(block * half, (block + 1) * half)
            out_ref[block ^ me, :, i * BASE : (i + 1) * BASE] = low[rows]
            out_ref[block ^ me, :, cols + i * BASE : cols + (i + 1) * BASE] = high[rows]


def first_rotation(where, own, got):
    blocks, half, cols = got.shape
    return pl.pallas_call(
        first_kernel,
        in_specs=[whole(pltpu.SMEM), whole(), whole()],
        out_specs=whole(),
        out_shape=jax.ShapeDtypeStruct((blocks, half, 2 * cols), got.dtype),
        compiler_params=pltpu.CompilerParams(vmem_limit_bytes=VMEM_LIMIT),
        cost_estimate=WORTH,
        name="first_rotation",
    )(where, own, got)


def rotate(order, norm, where_ref, held_ref, got_ref, send_ref, scale_ref, work):
    d1, d2, d3 = order
    place = {}
    for ref, base in ((held_ref, 0), (got_ref, d3)):
        for j, other in enumerate((0, d1, d2, d2 ^ d1)):
            place[base ^ other] = (ref, j)
    cols = held_ref.shape[-1]
    me = where_ref[1]

    def step(unit, carry):
        rows = pl.ds(pl.multiple_of(unit * UNIT, UNIT), UNIT)
        peak = None
        for c in range(0, cols, LANES):
            parts = butterfly(
                place[i][0][place[i][1], rows, c : c + LANES].astype(jnp.float32)
                for i in range(GROUPS)
            )
            for k, part in enumerate(parts):
                work[k, :, c : c + LANES] = part
                part = jnp.abs(part)
                peak = part if peak is None else jnp.maximum(peak, part)
        scale = jnp.max(peak, axis=1, keepdims=True) * norm + 1e-06
        scale_ref[rows, :] = jnp.broadcast_to(scale, (UNIT, EXTRA))
        factor = norm / scale
        for k in range(GROUPS):
            signed = factor * jnp.where(odd_bits(me & k, 3) == 0, 1.0, -1.0).astype(jnp.float32)
            for c in range(0, cols, LANES):
                value = (work[k, :, c : c + LANES] * signed).astype(send_ref.dtype)
                send_ref[rows, k * cols + c : k * cols + c + LANES] = value
        high = scale.astype(jnp.bfloat16).astype(jnp.float32)
        mid = (scale - high).astype(jnp.bfloat16).astype(jnp.float32)
        low = scale - high - mid
        lane = lax.broadcasted_iota(jnp.int32, (UNIT, EXTRA), 1)
        terms = jnp.where(lane == 0, high, jnp.where(lane == 1, mid, low))
        send_ref[rows, GROUPS * cols :] = terms.astype(send_ref.dtype)
        return carry

    lax.fori_loop(0, held_ref.shape[1] // UNIT, step, 0)


def places(where_ref, pieces, half, side):
    core = where_ref[0] if side == 0 else 1 - where_ref[0]
    for j, piece in enumerate(pieces):
        start = (where_ref[2] ^ piece) * (2 * half) + core * half
        yield slice(j * half, (j + 1) * half), pl.ds(pl.multiple_of(start, half), half)


def codes_kernel(order, norm, stored, half, earlier, chained, where_ref, *refs):
    refs = list(refs)

    def take(count):
        taken, refs[:] = refs[:count], refs[count:]
        return taken

    inputs = take(2 if order else 0)
    code_refs = take(len(stored))
    scales = take(len(earlier))
    take(1 if chained else 0)
    outputs = take(2 if order else 0)
    copies, got_scales = [], []
    if stored:
        (out_ref,) = take(1)
        wide = out_ref.shape[1]
        sems = refs[-1]
        for (pieces, side), ref in zip(stored, code_refs):
            for rows, place in places(where_ref, pieces, half, side):
                copies.append(
                    pltpu.make_async_copy(
                        ref.at[rows, pl.ds(0, wide)], out_ref.at[place], sems.at[len(copies)]
                    )
                )
        for copy in copies:
            copy.start()
        for (pieces, side), ref in zip(stored, code_refs):
            if side == 1:
                terms = ref[:, wide:].astype(jnp.float32)
                scale = (terms[:, :1] + terms[:, 1:2]) + terms[:, 2:3]
                scale = jnp.broadcast_to(scale, (scale.shape[0], EXTRA))
                got_scales.append((pieces, scale))
    got_scale_refs = take(1 if earlier else len(got_scales))
    if order:
        rotate(order, norm, where_ref, *inputs, *outputs, *take(1))
    if earlier:
        (table,) = take(1)
        for (pieces, side), ref in zip(earlier, scales):
            for rows, place in places(where_ref, pieces, half, side):
                table[place, :] = ref[rows, :]
        for pieces, scale in got_scales:
            for rows, place in places(where_ref, pieces, half, 1):
                table[place, :] = scale[rows]
        shape = (EXTRA, EXTRA)
        row, lane = (lax.broadcasted_iota(jnp.int32, shape, axis) for axis in range(2))
        (scale_ref,) = got_scale_refs
        for q in range(scale_ref.shape[0]):
            block = table[q * EXTRA : (q + 1) * EXTRA, :]
            line = jnp.sum(jnp.where(row == lane, block, 0.0), axis=0, keepdims=True)
            scale_ref[q : q + 1, :] = line
    else:
        for ref, (_, scale) in zip(got_scale_refs, got_scales):
            ref[...] = scale
    for copy in copies:
        copy.wait()


def codes_call(order, norm, inputs, stored, parts, earlier, scales, out, where, half, full):
    dtype = jnp.bfloat16
    operands = [where, *inputs, *parts, *scales]
    in_specs = [whole(pltpu.SMEM)] + [whole()] * (len(operands) - 1)
    out_specs, out_shape, scratch, aliases = [], [], [], {}
    moved = 0
    if order:
        _, rows, cols = inputs[0].shape
        moved = rows // half
        out_specs += [whole(), whole()]
        out_shape += [
            jax.ShapeDtypeStruct((rows, GROUPS * cols + EXTRA), dtype),
            jax.ShapeDtypeStruct((rows, EXTRA), jnp.float32),
        ]
        scratch.append(pltpu.VMEM((GROUPS, UNIT, cols), jnp.float32))
    if earlier:
        scratch.append(pltpu.VMEM((full, EXTRA), jnp.float32))
    if stored:
        if out is not None:
            aliases = {len(operands): len(out_shape)}
            in_specs.append(whole(pl.ANY))
            operands.append(out)
        out_specs.append(whole(pl.ANY))
        out_shape.append(jax.ShapeDtypeStruct((full, parts[0].shape[1] - EXTRA), dtype))
        scratch.append(pltpu.SemaphoreType.DMA((sum(len(pieces) for pieces, _ in stored),)))
    heights = [part.shape[0] for part, (_, side) in zip(parts, stored) if side == 1]
    if earlier:
        heights = [full // EXTRA]
    out_specs += [whole()] * len(heights)
    out_shape += [jax.ShapeDtypeStruct((height, EXTRA), jnp.float32) for height in heights]
    return pl.pallas_call(
        functools.partial(codes_kernel, order, norm, stored, half, earlier, bool(aliases)),
        in_specs=in_specs,
        out_specs=out_specs,
        out_shape=out_shape,
        scratch_shapes=scratch,
        input_output_aliases=aliases,
        compiler_params=pltpu.CompilerParams(vmem_limit_bytes=VMEM_LIMIT),
        cost_estimate=WORTH,
        name=f"rotate{moved}_store{sum(len(pieces) for pieces, _ in stored)}",
    )(*operands)


def local(weight):
    position = lax.axis_index("col")
    core = position % 2
    row = lax.axis_index("row")
    where = jnp.stack([core, position // 2, row])
    rows, cols = weight.shape
    blocks = lax.axis_size("row")
    block = rows // blocks
    half = block // 2
    norm = 1.0 / float(np.sqrt(cols * lax.axis_size("col")))

    weight = weight.reshape(blocks, block, cols)
    send = lax.dynamic_slice_in_dim(weight, (1 - core) * half, half, axis=1)
    own = lax.dynamic_slice_in_dim(weight, core * half, half, axis=1)
    part = first_rotation(where, own, swapped(send, "col", 1))

    token = part

    def after(value):
        return lax.optimization_barrier((value, token))[0]

    pieces = {0: part[0], 1: part[1]}
    held, got, taken = {}, {}, {}
    scales = {}
    codes = None
    for step in PLAN:
        kind, i = step[0], int(step[1:2])
        if kind == "z":
            token = after(part[i : i + 2])
            pair = swapped(token, "row", i)
            pieces[i], pieces[i + 1] = pair[0], pair[1]
            continue
        names, order = CHUNKS[i] if kind not in "or" else ((), ())
        order = [STEPS[name] for name in order]
        if kind == "m":
            token = after(jnp.concatenate([pieces[name] for name in names])[None])
            held[i], got[i] = from_neighbours(token)
            taken[i] = 1
        elif kind == "g":
            turn = taken.get(i, 0)
            taken[i] = turn + 1
            if turn == 0:
                held[i] = jnp.concatenate([pieces[name] for name in names])[None]
            else:
                held[i] = jnp.concatenate([held[i], got[i]])
            token = held[i] = after(held[i])
            got[i] = swapped(token, "col", 2 * order[turn])
        else:
            named, side = [], 0
            for letter in step[2 * (kind == "k") :]:
                if letter in "or":
                    side = "or".index(letter)
                else:
                    named.append((int(letter), side))
            stored = [(CHUNKS[c][0], side) for c, side in named]
            parts = [(held, got)[side][c] for c, side in named]
            earlier = dict(scales) if step == PLAN[-1] else {}
            inputs = ()
            if kind == "k":
                inputs = (held[i], after(got[i]))
            else:
                parts[-1] = after(parts[-1])
            made = codes_call(
                order,
                norm,
                inputs,
                stored,
                parts,
                list(earlier),
                list(earlier.values()),
                codes,
                where,
                half,
                rows,
            )
            if kind == "k":
                held[i], scales[names, 0], *made = made
                got[i] = swapped(held[i], "col", 1)
                token = held[i]
            if stored:
                codes, *made = made
                got_pieces = [pieces_of for pieces_of, side in stored if side == 1]
                for pieces_of, scale in zip(got_pieces, made):
                    scales[pieces_of, 1] = scale

    return codes, made[0].reshape(rows)


def solution(mesh):
    return jax.shard_map(
        local,
        mesh=mesh,
        in_specs=(P("row", "col"),),
        out_specs=(P("row", None), P("row")),
        check_vma=False,
    )
```

```python
import functools

import jax
import jax.numpy as jnp
import numpy as np
from jax import lax
from jax.experimental import pallas as pl
from jax.experimental.pallas import tpu as pltpu
from jax.sharding import PartitionSpec as P

UNIT = 16
LANES = 256
BASE = 256
EXTRA = 128
GROUPS = 8
VMEM_LIMIT = 12 * 2**20
WORTH = pl.CostEstimate(flops=2*10**10, bytes_accessed=1, transcendentals=0)

STEPS = {"a": 1, "b": 3, "y": 4}


CHUNKS = (
    ((0,), "aby"),
    ((2, 6), "bay"),
    ((1,), "yba"),
    ((4,), "ayb"),
    ((3, 7), "yba"),
    ((5,), "yab"),
)

PLAN = (
    "z2", "m2", "z6", "z4", "g1", "g0", "g1", "g0", "m4", "g3", "m5", "g3", "g2", "g5", "g4",
    "g2", "g0", "g3", "g1", "g4", "g5", "k0", "k2o0", "k5o2", "k3o5", "k1o3r02", "k4o1r53",
    "o4r1", "r4",
)


def swapped(value, axis, mask):
    pairs = [(source, source ^ mask) for source in range(lax.axis_size(axis))]
    return lax.ppermute(value, axis, pairs)


def from_neighbours(value):
    height = lax.axis_size("row")
    far = 2 * STEPS["y"] * height + 1
    pairs = [(source, source ^ far) for source in range(lax.axis_size("col") * height)]
    return swapped(value, "row", 1), lax.ppermute(value, ("col", "row"), pairs)


def butterfly(parts):
    parts = list(parts)
    span = 1
    while span < len(parts):
        for i in range(len(parts)):
            if not i & span:
                a, b = parts[i], parts[i | span]
                parts[i], parts[i | span] = a + b, a - b
        span *= 2
    return parts


def whole(space=pltpu.VMEM):
    return pl.BlockSpec(memory_space=space)


def odd_bits(value, bits):
    total = value
    for bit in range(1, bits):
        total = total ^ (value >> bit)
    return total & 1


def first_kernel(where_ref, own_ref, got_ref, out_ref):
    sign = jnp.where(where_ref[0] == 0, 1.0, -1.0).astype(jnp.float32)
    me = where_ref[2]
    blocks, half, cols = got_ref.shape
    shape = (BASE, BASE)
    both = lax.broadcasted_iota(jnp.int32, shape, 0) & lax.broadcasted_iota(jnp.int32, shape, 1)
    both = both ^ (both >> 4)
    both = both ^ (both >> 2)
    both = both ^ (both >> 1)
    table = (1 - 2 * (both & 1)).astype(jnp.float32).astype(jnp.bfloat16)

    def rotated(value):
        value = value.reshape(blocks * half, cols)
        return butterfly(
            jnp.dot(value[:, c : c + BASE], table, preferred_element_type=jnp.float32)
            for c in range(0, cols, BASE)
        )

    for i, (a, b) in enumerate(zip(rotated(own_ref[...]), rotated(got_ref[...]))):
        low = (a + b).astype(out_ref.dtype)
        high = ((a - b) * sign).astype(out_ref.dtype)
        for block in range(blocks):
            rows = slice(block * half, (block + 1) * half)
            out_ref[block ^ me, :, i * BASE : (i + 1) * BASE] = low[rows]
            out_ref[block ^ me, :, cols + i * BASE : cols + (i + 1) * BASE] = high[rows]


def first_rotation(where, own, got):
    blocks, half, cols = got.shape
    return pl.pallas_call(
        first_kernel,
        in_specs=[whole(pltpu.SMEM), whole(), whole()],
        out_specs=whole(),
        out_shape=jax.ShapeDtypeStruct((blocks, half, 2 * cols), got.dtype),
        compiler_params=pltpu.CompilerParams(vmem_limit_bytes=VMEM_LIMIT),
        cost_estimate=WORTH,
        name="first_rotation",
    )(where, own, got)


def rotate(order, norm, where_ref, held_ref, got_ref, send_ref, scale_ref, work):
    d1, d2, d3 = order
    place = {}
    for ref, base in ((held_ref, 0), (got_ref, d3)):
        for j, other in enumerate((0, d1, d2, d2 ^ d1)):
            place[base ^ other] = (ref, j)
    cols = held_ref.shape[-1]
    me = where_ref[1]

    def step(unit, carry):
        rows = pl.ds(pl.multiple_of(unit * UNIT, UNIT), UNIT)
        peak = None
        for c in range(0, cols, LANES):
            parts = butterfly(
                place[i][0][place[i][1], rows, c : c + LANES].astype(jnp.float32)
                for i in range(GROUPS)
            )
            for k, part in enumerate(parts):
                work[k, :, c : c + LANES] = part
                part = jnp.abs(part)
                peak = part if peak is None else jnp.maximum(peak, part)
        scale = jnp.max(peak, axis=1, keepdims=True) * norm + 1e-06
        scale_ref[rows, :] = jnp.broadcast_to(scale, (UNIT, EXTRA))
        factor = norm / scale
        for k in range(GROUPS):
            signed = factor * jnp.where(odd_bits(me & k, 3) == 0, 1.0, -1.0).astype(jnp.float32)
            for c in range(0, cols, LANES):
                value = (work[k, :, c : c + LANES] * signed).astype(send_ref.dtype)
                send_ref[rows, k * cols + c : k * cols + c + LANES] = value
        high = scale.astype(jnp.bfloat16).astype(jnp.float32)
        mid = (scale - high).astype(jnp.bfloat16).astype(jnp.float32)
        low = scale - high - mid
        lane = lax.broadcasted_iota(jnp.int32, (UNIT, EXTRA), 1)
        terms = jnp.where(lane == 0, high, jnp.where(lane == 1, mid, low))
        send_ref[rows, GROUPS * cols :] = terms.astype(send_ref.dtype)
        return carry

    lax.fori_loop(0, held_ref.shape[1] // UNIT, step, 0)


def places(where_ref, pieces, half, side):
    core = where_ref[0] if side == 0 else 1 - where_ref[0]
    for j, piece in enumerate(pieces):
        start = (where_ref[2] ^ piece) * (2 * half) + core * half
        yield slice(j * half, (j + 1) * half), pl.ds(pl.multiple_of(start, half), half)


def codes_kernel(order, norm, stored, half, earlier, chained, where_ref, *refs):
    refs = list(refs)

    def take(count):
        taken, refs[:] = refs[:count], refs[count:]
        return taken

    inputs = take(2 if order else 0)
    code_refs = take(len(stored))
    scales = take(len(earlier))
    take(1 if chained else 0)
    outputs = take(2 if order else 0)
    copies, got_scales = [], []
    if stored:
        (out_ref,) = take(1)
        wide = out_ref.shape[1]
        sems = refs[-1]
        for (pieces, side), ref in zip(stored, code_refs):
            for rows, place in places(where_ref, pieces, half, side):
                copies.append(
                    pltpu.make_async_copy(
                        ref.at[rows, pl.ds(0, wide)], out_ref.at[place], sems.at[len(copies)]
                    )
                )
        for copy in copies:
            copy.start()
        for (pieces, side), ref in zip(stored, code_refs):
            if side == 1:
                terms = ref[:, wide:].astype(jnp.float32)
                scale = (terms[:, :1] + terms[:, 1:2]) + terms[:, 2:3]
                scale = jnp.broadcast_to(scale, (scale.shape[0], EXTRA))
                got_scales.append((pieces, scale))
    got_scale_refs = take(1 if earlier else len(got_scales))
    if order:
        rotate(order, norm, where_ref, *inputs, *outputs, *take(1))
    if earlier:
        (table,) = take(1)
        for (pieces, side), ref in zip(earlier, scales):
            for rows, place in places(where_ref, pieces, half, side):
                table[place, :] = ref[rows, :]
        for pieces, scale in got_scales:
            for rows, place in places(where_ref, pieces, half, 1):
                table[place, :] = scale[rows]
        shape = (EXTRA, EXTRA)
        row, lane = (lax.broadcasted_iota(jnp.int32, shape, axis) for axis in range(2))
        (scale_ref,) = got_scale_refs
        for q in range(scale_ref.shape[0]):
            block = table[q * EXTRA : (q + 1) * EXTRA, :]
            line = jnp.sum(jnp.where(row == lane, block, 0.0), axis=0, keepdims=True)
            scale_ref[q : q + 1, :] = line
    else:
        for ref, (_, scale) in zip(got_scale_refs, got_scales):
            ref[...] = scale
    for copy in copies:
        copy.wait()


def codes_call(order, norm, inputs, stored, parts, earlier, scales, out, where, half, full):
    dtype = jnp.bfloat16
    operands = [where, *inputs, *parts, *scales]
    in_specs = [whole(pltpu.SMEM)] + [whole()] * (len(operands) - 1)
    out_specs, out_shape, scratch, aliases = [], [], [], {}
    moved = 0
    if order:
        _, rows, cols = inputs[0].shape
        moved = rows // half
        out_specs += [whole(), whole()]
        out_shape += [
            jax.ShapeDtypeStruct((rows, GROUPS * cols + EXTRA), dtype),
            jax.ShapeDtypeStruct((rows, EXTRA), jnp.float32),
        ]
        scratch.append(pltpu.VMEM((GROUPS, UNIT, cols), jnp.float32))
    if earlier:
        scratch.append(pltpu.VMEM((full, EXTRA), jnp.float32))
    if stored:
        if out is not None:
            aliases = {len(operands): len(out_shape)}
            in_specs.append(whole(pl.ANY))
            operands.append(out)
        out_specs.append(whole(pl.ANY))
        out_shape.append(jax.ShapeDtypeStruct((full, parts[0].shape[1] - EXTRA), dtype))
        scratch.append(pltpu.SemaphoreType.DMA((sum(len(pieces) for pieces, _ in stored),)))
    heights = [part.shape[0] for part, (_, side) in zip(parts, stored) if side == 1]
    if earlier:
        heights = [full // EXTRA]
    out_specs += [whole()] * len(heights)
    out_shape += [jax.ShapeDtypeStruct((height, EXTRA), jnp.float32) for height in heights]
    return pl.pallas_call(
        functools.partial(codes_kernel, order, norm, stored, half, earlier, bool(aliases)),
        in_specs=in_specs,
        out_specs=out_specs,
        out_shape=out_shape,
        scratch_shapes=scratch,
        input_output_aliases=aliases,
        compiler_params=pltpu.CompilerParams(vmem_limit_bytes=VMEM_LIMIT),
        cost_estimate=WORTH,
        name=f"rotate{moved}_store{sum(len(pieces) for pieces, _ in stored)}",
    )(*operands)


def local(weight):
    position = lax.axis_index("col")
    core = position % 2
    row = lax.axis_index("row")
    where = jnp.stack([core, position // 2, row])
    rows, cols = weight.shape
    blocks = lax.axis_size("row")
    block = rows // blocks
    half = block // 2
    norm = 1.0 / float(np.sqrt(cols * lax.axis_size("col")))

    weight = weight.reshape(blocks, block, cols)
    send = lax.dynamic_slice_in_dim(weight, (1 - core) * half, half, axis=1)
    own = lax.dynamic_slice_in_dim(weight, core * half, half, axis=1)
    part = first_rotation(where, own, swapped(send, "col", 1))

    token = part

    def after(value):
        return lax.optimization_barrier((value, token))[0]

    pieces = {0: part[0], 1: part[1]}
    held, got, taken = {}, {}, {}
    scales = {}
    codes = None
    for step in PLAN:
        kind, i = step[0], int(step[1:2])
        if kind == "z":
            token = after(part[i : i + 2])
            pair = swapped(token, "row", i)
            pieces[i], pieces[i + 1] = pair[0], pair[1]
            continue
        names, order = CHUNKS[i] if kind not in "or" else ((), ())
        order = [STEPS[name] for name in order]
        if kind == "m":
            token = after(jnp.concatenate([pieces[name] for name in names])[None])
            held[i], got[i] = from_neighbours(token)
            taken[i] = 1
        elif kind == "g":
            turn = taken.get(i, 0)
            taken[i] = turn + 1
            if turn == 0:
                held[i] = jnp.concatenate([pieces[name] for name in names])[None]
            else:
                held[i] = jnp.concatenate([held[i], got[i]])
            token = held[i] = after(held[i])
            got[i] = swapped(token, "col", 2 * order[turn])
        else:
            named, side = [], 0
            for letter in step[2 * (kind == "k") :]:
                if letter in "or":
                    side = "or".index(letter)
                else:
                    named.append((int(letter), side))
            stored = [(CHUNKS[c][0], side) for c, side in named]
            parts = [(held, got)[side][c] for c, side in named]
            earlier = dict(scales) if step == PLAN[-1] else {}
            inputs = ()
            if kind == "k":
                inputs = (held[i], after(got[i]))
            else:
                parts[-1] = after(parts[-1])
            made = codes_call(
                order,
                norm,
                inputs,
                stored,
                parts,
                list(earlier),
                list(earlier.values()),
                codes,
                where,
                half,
                rows,
            )
            if kind == "k":
                held[i], scales[names, 0], *made = made
                got[i] = swapped(held[i], "col", 1)
                token = held[i]
            if stored:
                codes, *made = made
                got_pieces = [pieces_of for pieces_of, side in stored if side == 1]
                for pieces_of, scale in zip(got_pieces, made):
                    scales[pieces_of, 1] = scale

    return codes, made[0].reshape(rows)


def solution(mesh):
    return jax.shard_map(
        local,
        mesh=mesh,
        in_specs=(P("row", "col"),),
        out_specs=(P("row", None), P("row")),
        check_vma=False,
    )
```

```python
import functools

import jax
import jax.numpy as jnp
import numpy as np
from jax import lax
from jax.experimental import pallas as pl
from jax.experimental.pallas import tpu as pltpu
from jax.sharding import PartitionSpec as P

UNIT = 16
LANES = 256
BASE = 256
EXTRA = 128
GROUPS = 8
VMEM_LIMIT = 12 * 2**20
WORTH = pl.CostEstimate(flops=2*10**10, bytes_accessed=1, transcendentals=0)

STEPS = {"a": 1, "b": 3, "y": 4}


CHUNKS = (
    ((0,), "aby"),
    ((2, 6), "bay"),
    ((1,), "yba"),
    ((4,), "ayb"),
    ((3, 7), "yba"),
    ((5,), "yab"),
)

PLAN = (
    "z2", "m2", "z6", "z4", "g1", "g0", "g1", "g0", "m4", "g3", "m5", "g3", "g2", "g5", "g4",
    "g2", "g0", "g3", "g1", "g4", "g5", "k0", "k2o0", "k5o2", "k3o5", "k1o3r02", "k4o1r53",
    "o4r1", "r4",
)


def swapped(value, axis, mask):
    pairs = [(source, source ^ mask) for source in range(lax.axis_size(axis))]
    return lax.ppermute(value, axis, pairs)


def from_neighbours(value):
    height = lax.axis_size("row")
    far = 2 * STEPS["y"] * height + 1
    pairs = [(source, source ^ far) for source in range(lax.axis_size("col") * height)]
    return swapped(value, "row", 1), lax.ppermute(value, ("col", "row"), pairs)


def butterfly(parts):
    parts = list(parts)
    span = 1
    while span < len(parts):
        for i in range(len(parts)):
            if not i & span:
                a, b = parts[i], parts[i | span]
                parts[i], parts[i | span] = a + b, a - b
        span *= 2
    return parts


def whole(space=pltpu.VMEM):
    return pl.BlockSpec(memory_space=space)


def odd_bits(value, bits):
    total = value
    for bit in range(1, bits):
        total = total ^ (value >> bit)
    return total & 1


def first_kernel(where_ref, own_ref, got_ref, out_ref):
    sign = jnp.where(where_ref[0] == 0, 1.0, -1.0).astype(jnp.float32)
    me = where_ref[2]
    blocks, half, cols = got_ref.shape
    shape = (BASE, BASE)
    both = lax.broadcasted_iota(jnp.int32, shape, 0) & lax.broadcasted_iota(jnp.int32, shape, 1)
    both = both ^ (both >> 4)
    both = both ^ (both >> 2)
    both = both ^ (both >> 1)
    table = (1 - 2 * (both & 1)).astype(jnp.float32).astype(jnp.bfloat16)

    def rotated(value):
        value = value.reshape(blocks * half, cols)
        return butterfly(
            jnp.dot(value[:, c : c + BASE], table, preferred_element_type=jnp.float32)
            for c in range(0, cols, BASE)
        )

    for i, (a, b) in enumerate(zip(rotated(own_ref[...]), rotated(got_ref[...]))):
        low = (a + b).astype(out_ref.dtype)
        high = ((a - b) * sign).astype(out_ref.dtype)
        for block in range(blocks):
            rows = slice(block * half, (block + 1) * half)
            out_ref[block ^ me, :, i * BASE : (i + 1) * BASE] = low[rows]
            out_ref[block ^ me, :, cols + i * BASE : cols + (i + 1) * BASE] = high[rows]


def first_rotation(where, own, got):
    blocks, half, cols = got.shape
    return pl.pallas_call(
        first_kernel,
        in_specs=[whole(pltpu.SMEM), whole(), whole()],
        out_specs=whole(),
        out_shape=jax.ShapeDtypeStruct((blocks, half, 2 * cols), got.dtype),
        compiler_params=pltpu.CompilerParams(vmem_limit_bytes=VMEM_LIMIT),
        cost_estimate=WORTH,
        name="first_rotation",
    )(where, own, got)


def rotate(order, norm, where_ref, held_ref, got_ref, send_ref, scale_ref, work):
    d1, d2, d3 = order
    place = {}
    for ref, base in ((held_ref, 0), (got_ref, d3)):
        for j, other in enumerate((0, d1, d2, d2 ^ d1)):
            place[base ^ other] = (ref, j)
    cols = held_ref.shape[-1]
    me = where_ref[1]

    def step(unit, carry):
        rows = pl.ds(pl.multiple_of(unit * UNIT, UNIT), UNIT)
        peak = None
        for c in range(0, cols, LANES):
            parts = butterfly(
                place[i][0][place[i][1], rows, c : c + LANES].astype(jnp.float32)
                for i in range(GROUPS)
            )
            for k, part in enumerate(parts):
                work[k, :, c : c + LANES] = part
                part = jnp.abs(part)
                peak = part if peak is None else jnp.maximum(peak, part)
        scale = jnp.max(peak, axis=1, keepdims=True) * norm + 1e-06
        scale_ref[rows, :] = jnp.broadcast_to(scale, (UNIT, EXTRA))
        factor = norm / scale
        for k in range(GROUPS):
            signed = factor * jnp.where(odd_bits(me & k, 3) == 0, 1.0, -1.0).astype(jnp.float32)
            for c in range(0, cols, LANES):
                value = (work[k, :, c : c + LANES] * signed).astype(send_ref.dtype)
                send_ref[rows, k * cols + c : k * cols + c + LANES] = value
        high = scale.astype(jnp.bfloat16).astype(jnp.float32)
        mid = (scale - high).astype(jnp.bfloat16).astype(jnp.float32)
        low = scale - high - mid
        lane = lax.broadcasted_iota(jnp.int32, (UNIT, EXTRA), 1)
        terms = jnp.where(lane == 0, high, jnp.where(lane == 1, mid, low))
        send_ref[rows, GROUPS * cols :] = terms.astype(send_ref.dtype)
        return carry

    lax.fori_loop(0, held_ref.shape[1] // UNIT, step, 0)


def places(where_ref, pieces, half, side):
    core = where_ref[0] if side == 0 else 1 - where_ref[0]
    for j, piece in enumerate(pieces):
        start = (where_ref[2] ^ piece) * (2 * half) + core * half
        yield slice(j * half, (j + 1) * half), pl.ds(pl.multiple_of(start, half), half)


def codes_kernel(order, norm, stored, half, earlier, chained, where_ref, *refs):
    refs = list(refs)

    def take(count):
        taken, refs[:] = refs[:count], refs[count:]
        return taken

    inputs = take(2 if order else 0)
    code_refs = take(len(stored))
    scales = take(len(earlier))
    take(1 if chained else 0)
    outputs = take(2 if order else 0)
    copies, got_scales = [], []
    if stored:
        (out_ref,) = take(1)
        wide = out_ref.shape[1]
        sems = refs[-1]
        for (pieces, side), ref in zip(stored, code_refs):
            for rows, place in places(where_ref, pieces, half, side):
                copies.append(
                    pltpu.make_async_copy(
                        ref.at[rows, pl.ds(0, wide)], out_ref.at[place], sems.at[len(copies)]
                    )
                )
        for copy in copies:
            copy.start()
        for (pieces, side), ref in zip(stored, code_refs):
            if side == 1:
                terms = ref[:, wide:].astype(jnp.float32)
                scale = (terms[:, :1] + terms[:, 1:2]) + terms[:, 2:3]
                scale = jnp.broadcast_to(scale, (scale.shape[0], EXTRA))
                got_scales.append((pieces, scale))
    got_scale_refs = take(1 if earlier else len(got_scales))
    if order:
        rotate(order, norm, where_ref, *inputs, *outputs, *take(1))
    if earlier:
        (scale_ref,) = got_scale_refs
        whole_table = scale_ref.shape[0] == 8 * half * 2
        table = scale_ref if whole_table else take(1)[0]
        if not whole_table:
            table[...] = scales[0][...]
        for (pieces, side), ref in zip(earlier, scales if whole_table else ()):
            for rows, place in places(where_ref, pieces, half, side):
                table[place, :] = ref[rows, :]
        for pieces, scale in got_scales:
            for rows, place in places(where_ref, pieces, half, 1):
                table[place, :] = scale[rows]
        shape = (EXTRA, EXTRA)
        row, lane = (lax.broadcasted_iota(jnp.int32, shape, axis) for axis in range(2))
        for q in range(0 if whole_table else scale_ref.shape[0]):
            block = table[q * EXTRA : (q + 1) * EXTRA, :]
            line = jnp.sum(jnp.where(row == lane, block, 0.0), axis=0, keepdims=True)
            scale_ref[q : q + 1, :] = line
    else:
        for ref, (_, scale) in zip(got_scale_refs, got_scales):
            ref[...] = scale
    for copy in copies:
        copy.wait()


def codes_call(order, norm, inputs, stored, parts, earlier, scales, out, where, half, full):
    dtype = jnp.bfloat16
    operands = [where, *inputs, *parts, *scales]
    in_specs = [whole(pltpu.SMEM)] + [whole()] * (len(operands) - 1)
    out_specs, out_shape, scratch, aliases = [], [], [], {}
    moved = 0
    if order:
        _, rows, cols = inputs[0].shape
        moved = rows // half
        out_specs += [whole(), whole()]
        out_shape += [
            jax.ShapeDtypeStruct((rows, GROUPS * cols + EXTRA), dtype),
            jax.ShapeDtypeStruct((rows, EXTRA), jnp.float32),
        ]
        scratch.append(pltpu.VMEM((GROUPS, UNIT, cols), jnp.float32))
    if earlier:
        scratch.append(pltpu.VMEM((full, EXTRA), jnp.float32))
    if stored:
        if out is not None:
            aliases = {len(operands): len(out_shape)}
            in_specs.append(whole(pl.ANY))
            operands.append(out)
        out_specs.append(whole(pl.ANY))
        out_shape.append(jax.ShapeDtypeStruct((full, parts[0].shape[1] - EXTRA), dtype))
        scratch.append(pltpu.SemaphoreType.DMA((sum(len(pieces) for pieces, _ in stored),)))
    heights = [part.shape[0] for part, (_, side) in zip(parts, stored) if side == 1]
    if earlier:
        heights = [full // EXTRA if len(earlier) == 1 else full]
    out_specs += [whole()] * len(heights)
    out_shape += [jax.ShapeDtypeStruct((height, EXTRA), jnp.float32) for height in heights]
    return pl.pallas_call(
        functools.partial(codes_kernel, order, norm, stored, half, earlier, bool(aliases)),
        in_specs=in_specs,
        out_specs=out_specs,
        out_shape=out_shape,
        scratch_shapes=scratch,
        input_output_aliases=aliases,
        compiler_params=pltpu.CompilerParams(vmem_limit_bytes=VMEM_LIMIT),
        cost_estimate=WORTH,
        name=f"rotate{moved}_store{sum(len(pieces) for pieces, _ in stored)}",
    )(*operands)


def local(weight):
    position = lax.axis_index("col")
    core = position % 2
    row = lax.axis_index("row")
    where = jnp.stack([core, position // 2, row])
    rows, cols = weight.shape
    blocks = lax.axis_size("row")
    block = rows // blocks
    half = block // 2
    norm = 1.0 / float(np.sqrt(cols * lax.axis_size("col")))

    weight = weight.reshape(blocks, block, cols)
    send = lax.dynamic_slice_in_dim(weight, (1 - core) * half, half, axis=1)
    own = lax.dynamic_slice_in_dim(weight, core * half, half, axis=1)
    part = first_rotation(where, own, swapped(send, "col", 1))

    token = part

    def after(value):
        return lax.optimization_barrier((value, token))[0]

    pieces = {0: part[0], 1: part[1]}
    held, got, taken = {}, {}, {}
    scales = {}
    codes = None
    for step in PLAN:
        kind, i = step[0], int(step[1:2])
        if kind == "z":
            token = after(part[i : i + 2])
            pair = swapped(token, "row", i)
            pieces[i], pieces[i + 1] = pair[0], pair[1]
            continue
        names, order = CHUNKS[i] if kind not in "or" else ((), ())
        order = [STEPS[name] for name in order]
        if kind == "m":
            token = after(jnp.concatenate([pieces[name] for name in names])[None])
            held[i], got[i] = from_neighbours(token)
            taken[i] = 1
        elif kind == "g":
            turn = taken.get(i, 0)
            taken[i] = turn + 1
            if turn == 0:
                held[i] = jnp.concatenate([pieces[name] for name in names])[None]
            else:
                held[i] = jnp.concatenate([held[i], got[i]])
            token = held[i] = after(held[i])
            got[i] = swapped(token, "col", 2 * order[turn])
        else:
            named, side = [], 0
            for letter in step[2 * (kind == "k") :]:
                if letter in "or":
                    side = "or".index(letter)
                else:
                    named.append((int(letter), side))
            stored = [(CHUNKS[c][0], side) for c, side in named]
            parts = [(held, got)[side][c] for c, side in named]
            earlier = dict(scales) if step in PLAN[-2:] else {}
            inputs = ()
            if kind == "k":
                inputs = (held[i], after(got[i]))
            else:
                parts[-1] = after(parts[-1])
            made = codes_call(
                order,
                norm,
                inputs,
                stored,
                parts,
                list(earlier),
                list(earlier.values()),
                codes,
                where,
                half,
                rows,
            )
            if kind == "k":
                held[i], scales[names, 0], *made = made
                got[i] = swapped(held[i], "col", 1)
                token = held[i]
            if stored:
                codes, *made = made
                got_pieces = [pieces_of for pieces_of, side in stored if side == 1]
                if earlier:
                    scales = {"all": made[0]}
                else:
                    for pieces_of, scale in zip(got_pieces, made):
                        scales[pieces_of, 1] = scale

    return codes, made[0].reshape(rows)


def solution(mesh):
    return jax.shard_map(
        local,
        mesh=mesh,
        in_specs=(P("row", "col"),),
        out_specs=(P("row", None), P("row")),
        check_vma=False,
    )
```
